32 devices in a mesh: emb: 8 (over z, y), seq: 4 (over x, core).
Axes of the slice: x: 2, y: 2, z: 4, core: 2. Of those that a mesh axis runs over, the one named last changes fastest.
Arguments:
- item_table: bfloat16 [32768, 512], P(('emb', 'seq')), may hold values from -6 to 6
- unique_ids: int32 [2048], P(('emb', 'seq')), may hold values from 0 to 32767, as said below
- inverse: int32 [256, 256], P(('emb', 'seq')), may hold values from 0 to 63, as said below
- lengths: int32 [256], P(('emb', 'seq')), may hold values from 64 to 256, as said below
- assignment: int32 [256], P(('emb', 'seq')), may hold values from 0 to 31, as said below
- proj_in: bfloat16 [512, 2048], replicated, may hold values from -0.25 to 0.25
- bias_in: float32 [2048], replicated, may hold values from -3 to 3
- gain_in: float32 [512], replicated, may hold values from 0.1 to 1.9
- gain_mid: float32 [512], replicated, may hold values from 0.1 to 1.9
- proj_out: bfloat16 [512, 512], replicated, may hold values from -0.25 to 0.25
- position_bias: float32 [4, 256], replicated, may hold values from -4 to 4
- cotangent: bfloat16 [256, 256, 512], P(('emb', 'seq')), may hold values from -6 to 6
Outputs:
- outputs: bfloat16 [256, 256, 512], P(('emb', 'seq'))
- table_grad: float32 [32768, 512], P(('emb', 'seq'))
The draws below stay inside these ranges and needn't reach their ends.
Inputs may be any that keep to these rules, and one draw needn't show every extreme that they name: `unique_ids`: each device's 64 entries are distinct row numbers; row r is held by device r // 1024; a device names at most 4 rows held by any one device, and exactly 4 of some device. `inverse`: every entry of a device's unique list is named by some token at a position below its slot's length. `lengths`: every group of 4 devices along seq has a slot of length 256. `assignment`: value v of a slot of a device with emb index e places it in slot v % 8 of the device with emb index e and seq index v // 8. Within a group it is a permutation, and the slots that the device with seq index s sends to a device take that device's slots s * 2 to (s + 1) * 2 - 1.
All inputs are finite; a program needn't handle non-finite values.
Results may differ from the reference program's by a relative error of at most 0.015.
Values may be sent and summed in bfloat16 or wider, within the bound.
A program may use at most 64 MiB of HBM per device.

```python
import jax
import jax.numpy as jnp
from jax import lax

D = 512
HEADS = 4
MAXLEN = 256
NSEQ = 8
ROWS_DEV = 1024
SLOTS = 4
UNIQ = 64
ROWS = 32768
SLOTS_ALL = 256
N_SEQ = 4
DEVICES = 32


def draw_unique_ids(key, part):
    stripe = ROWS_DEV // SLOTS

    def per_device(dev_key):
        key_off, key_pick, key_full, key_order = jax.random.split(dev_key, 4)
        offsets = jax.random.randint(key_off, (DEVICES, SLOTS), 0, stripe)
        local_rows = jnp.arange(SLOTS, dtype=jnp.int32)[None, :] * stripe + offsets
        id_grid = jnp.arange(DEVICES, dtype=jnp.int32)[:, None] * ROWS_DEV + local_rows
        scores = jax.random.randint(key_pick, (DEVICES, SLOTS), 0, 1 << 16) * (DEVICES * SLOTS)
        scores = scores + jnp.arange(DEVICES * SLOTS, dtype=jnp.int32).reshape(DEVICES, SLOTS)
        full_owner = jax.random.randint(key_full, (), 0, DEVICES)
        boosted = jnp.arange(DEVICES, dtype=jnp.int32)[:, None] == full_owner
        scores = jnp.where(boosted, scores + (1 << 16) * (DEVICES * SLOTS), scores)
        picked = lax.top_k(scores.reshape(-1), UNIQ)[1]
        chosen_ids = id_grid.reshape(-1)[picked]
        return chosen_ids[jax.random.permutation(key_order, UNIQ)]
    device_keys = jax.vmap(lambda device: jax.random.fold_in(key, device))(jnp.arange(DEVICES))
    return jax.vmap(per_device)(device_keys).reshape(-1).astype(jnp.int32)


def draw_inverse(key, part):
    early = MAXLEN // 4

    def per_device(dev_key):
        random_key_root, key_perm = jax.random.split(dev_key)
        base = jax.random.randint(random_key_root, (NSEQ, MAXLEN), 0, UNIQ)
        order = jax.random.permutation(key_perm, UNIQ)
        flat = jnp.arange(NSEQ, dtype=jnp.int32)[:, None] * early + jnp.arange(MAXLEN, dtype=jnp.int32)[None, :]
        forced = (jnp.arange(MAXLEN, dtype=jnp.int32)[None, :] < early) & (flat < UNIQ)
        return jnp.where(forced, order[jnp.minimum(flat, UNIQ - 1)], base)
    device_keys = jax.vmap(lambda device: jax.random.fold_in(key, device))(jnp.arange(DEVICES))
    return jax.vmap(per_device)(device_keys).reshape(DEVICES * NSEQ, MAXLEN).astype(jnp.int32)


def slot_plan(key):
    plan_key = jax.random.fold_in(key, 7)
    groups = DEVICES // N_SEQ
    key_heavy, key_long, key_short, key_top = jax.random.split(plan_key, 4)
    heavy = jax.random.randint(key_heavy, (groups,), 0, N_SEQ)
    long_len = jax.random.randint(key_long, (groups, N_SEQ, NSEQ), MAXLEN // 2, MAXLEN + 1)
    short_len = jax.random.randint(key_short, (groups, N_SEQ, NSEQ), MAXLEN // 4, MAXLEN // 2 + 1)
    is_heavy = jnp.arange(N_SEQ, dtype=jnp.int32)[None, :, None] == heavy[:, None, None]
    slot_lens = jnp.where(is_heavy, long_len, short_len)
    top_slot = jax.random.randint(key_top, (groups,), 0, NSEQ)
    is_top = is_heavy & (jnp.arange(NSEQ, dtype=jnp.int32)[None, None, :] == top_slot[:, None, None])
    slot_lens = jnp.where(is_top, MAXLEN, slot_lens)
    order_key = (MAXLEN - slot_lens) * NSEQ + jnp.arange(NSEQ, dtype=jnp.int32)[None, None, :]
    order = jnp.argsort(order_key, axis=-1)
    slot_rank = jnp.argsort(order, axis=-1).astype(jnp.int32)
    source = jnp.arange(N_SEQ, dtype=jnp.int32)[None, :, None]
    target = (source + slot_rank) % N_SEQ
    per_partner = NSEQ // N_SEQ
    placed = target * NSEQ + source * per_partner + slot_rank // N_SEQ
    return (slot_lens.reshape(-1).astype(jnp.int32), placed.reshape(-1).astype(jnp.int32))


def draw_lengths(key, part):
    return slot_plan(key)[0]


def draw_assignment(key, part):
    return slot_plan(key)[1]


def shard_levels(own_key, extent, shards, least, high):
    level = 1.0
    for axis_at, shards_of in shards:
        heights = jax.random.uniform(jax.random.fold_in(jax.random.fold_in(own_key, 6), axis_at), (shards_of,), jnp.float32, least / len(shards), high / len(shards))
        level = level * jnp.repeat(jnp.exp(heights), extent[axis_at] // shards_of).reshape((-1,) + (1,) * (len(extent) - 1 - axis_at))
    return level


def scatter_about(own_key, extent, width, reach, shards=(), held_as=jnp.bfloat16):
    values = width * jax.random.normal(own_key, extent, jnp.float32)
    if shards:
        values = values * shard_levels(own_key, extent, shards, -0.22, 0.18)
    return jnp.clip(values, -reach, reach).astype(held_as)


def setup_inputs(seed: int = 0) -> dict:
    keys = jax.random.split(jax.random.key(seed), 13)
    return {
        "item_table": scatter_about(keys[0], (ROWS, D), 1.0, 6.0, ((0, 32),)),
        "unique_ids": draw_unique_ids(jax.random.fold_in(keys[12], 71), 0),
        "inverse": draw_inverse(jax.random.fold_in(keys[12], 71), 0),
        "lengths": draw_lengths(jax.random.fold_in(keys[12], 71), 0),
        "assignment": draw_assignment(jax.random.fold_in(keys[12], 71), 0),
        "proj_in": scatter_about(keys[5], (D, 4 * D), D ** -0.5, 0.25),
        "bias_in": scatter_about(keys[6], (4 * D,), 0.5, 3.0, (), jnp.float32),
        "gain_in": jnp.clip(1.0 + 0.18 * jax.random.normal(keys[7], (D,), jnp.float32), 0.1, 1.9),
        "gain_mid": jnp.clip(1.0 + 0.18 * jax.random.normal(keys[8], (D,), jnp.float32), 0.1, 1.9),
        "proj_out": scatter_about(keys[9], (D, D), D ** -0.5, 0.25),
        "position_bias": scatter_about(keys[10], (HEADS, MAXLEN), 1.0, 4.0, (), jnp.float32),
        "cotangent": scatter_about(keys[11], (SLOTS_ALL, MAXLEN, D), 1.0, 6.0, ((0, 32),)),
    }


def layer_norm(values, gain):
    center = values - lax.optimization_barrier(jnp.mean(values, axis=-1, keepdims=True))
    spread = lax.optimization_barrier(jnp.mean(center * center, axis=-1, keepdims=True))
    return center * lax.rsqrt(spread + 1e-05) * gain

def relative_table(position_bias, length):
    row_pos = jnp.arange(length, dtype=jnp.int32)
    distance = jnp.clip(row_pos[:, None] - row_pos[None, :], 0, length - 1)
    return position_bias[:, distance]

def slot_layer(inputs, seq_len, proj_in, bias_in, gain_in, gain_mid, proj_out, toeplitz):
    length = inputs.shape[0]
    feature = inputs.shape[1]
    head_count = toeplitz.shape[0]
    head_size = feature // head_count
    normed = layer_norm(inputs.astype(jnp.float32), gain_in).astype(jnp.bfloat16)
    hidden = jax.nn.silu(jnp.dot(normed, proj_in, preferred_element_type=jnp.float32) + bias_in).astype(jnp.bfloat16)
    gate_portion = hidden[:, :feature]
    value_part = hidden[:, feature:2 * feature].reshape(length, head_count, head_size).astype(jnp.float32)
    query_part = hidden[:, 2 * feature:3 * feature].reshape(length, head_count, head_size).astype(jnp.float32)
    key_part = hidden[:, 3 * feature:].reshape(length, head_count, head_size).astype(jnp.float32)
    scores = jnp.einsum('ihe,jhe->hij', query_part, key_part) * head_size ** (-0.5) + toeplitz
    row_pos = jnp.arange(length, dtype=jnp.int32)[:, None]
    col_pos = jnp.arange(length, dtype=jnp.int32)[None, :]
    allowed = (col_pos <= row_pos) & (row_pos < seq_len)
    weights = jnp.where(allowed[None], jax.nn.silu(scores) / seq_len.astype(jnp.float32), 0.0).astype(jnp.bfloat16)
    mixed_heads = jnp.einsum('hij,jhe->ihe', weights.astype(jnp.float32), value_part).reshape(length, feature)
    gated_out = (layer_norm(mixed_heads, gain_mid) * gate_portion.astype(jnp.float32)).astype(jnp.bfloat16)
    result = inputs.astype(jnp.float32) + jnp.dot(gated_out, proj_out, preferred_element_type=jnp.float32)
    return jnp.where(row_pos < seq_len, result, 0.0).astype(jnp.bfloat16)

def slot_step(slot_in, seq_len, grad_out, proj_in, bias_in, gain_in, gain_mid, proj_out, toeplitz):
    result, pullback = jax.vjp(lambda inputs: slot_layer(inputs, seq_len, proj_in, bias_in, gain_in, gain_mid, proj_out, toeplitz), slot_in)
    return (result, pullback(grad_out)[0])

def reference(item_table, unique_ids, inverse, lengths, assignment, proj_in, bias_in, gain_in, gain_mid, proj_out, position_bias, cotangent):
    fetched = item_table[unique_ids]
    slot_total = DEVICES * NSEQ
    device_of = jnp.arange(slot_total, dtype=jnp.int32) // NSEQ
    token_ids = inverse + (device_of * UNIQ)[:, None]
    position = jnp.arange(MAXLEN, dtype=jnp.int32)
    in_range = position[None, :] < lengths[:, None]
    home_rows = jnp.where(in_range[:, :, None], fetched[token_ids], jnp.zeros((), jnp.bfloat16))
    destination = device_of // N_SEQ * (N_SEQ * NSEQ) + assignment
    balanced = jnp.zeros_like(home_rows).at[destination].set(home_rows)
    count_totals = jnp.zeros((slot_total,), jnp.int32).at[destination].set(lengths)
    toeplitz = relative_table(position_bias, MAXLEN)
    outputs, token_grads = lax.map(lambda packed: slot_step(packed[0], packed[1], packed[2], proj_in, bias_in, gain_in, gain_mid, proj_out, toeplitz), (balanced, count_totals, cotangent))
    home_grads = token_grads[destination].astype(jnp.float32)
    row_gradient_list = jnp.zeros((DEVICES * UNIQ, D), jnp.float32).at[token_ids].add(home_grads)
    table_grad = jnp.zeros((ROWS_DEV * DEVICES, D), jnp.float32).at[unique_ids].add(row_gradient_list)
    return (outputs, table_grad)
```

```python
import jax
import jax.numpy as jnp
from jax import lax
from jax.sharding import PartitionSpec as P


def layer_norm(values, gain):
    center = values - jnp.mean(values, axis=-1, keepdims=True)
    spread = jnp.mean(center * center, axis=-1, keepdims=True)
    return center * lax.rsqrt(spread + 1e-05) * gain


def relative_table(position_bias, length):
    head_count = position_bias.shape[0]
    first = jnp.broadcast_to(position_bias[:, :1], (head_count, length + 1))
    wrapped = jnp.concatenate([first, position_bias[:, :0:-1]], axis=1)
    tiled = jnp.tile(wrapped, (1, length))[:, : length * (2 * length - 1)]
    return tiled.reshape(head_count, length, 2 * length - 1)[:, :, :length]


def slot_layer(inputs, seq_len, proj_in, bias_in, gain_in, gain_mid, proj_out, toeplitz):
    length = inputs.shape[0]
    feature = inputs.shape[1]
    head_count = toeplitz.shape[0]
    head_size = feature // head_count
    normed = layer_norm(inputs.astype(jnp.float32), gain_in).astype(jnp.bfloat16)
    hidden = jax.nn.silu(
        jnp.dot(normed, proj_in, preferred_element_type=jnp.float32) + bias_in
    ).astype(jnp.bfloat16)
    gate_portion = hidden[:, :feature]
    value_part = hidden[:, feature : 2 * feature].reshape(length, head_count, head_size)
    query_part = hidden[:, 2 * feature : 3 * feature].reshape(length, head_count, head_size)
    key_part = hidden[:, 3 * feature :].reshape(length, head_count, head_size)
    scores = (
        jnp.einsum("ihe,jhe->hij", query_part, key_part, preferred_element_type=jnp.float32)
        * head_size ** (-0.5)
        + toeplitz
    )
    row_pos = jnp.arange(length, dtype=jnp.int32)[:, None]
    col_pos = jnp.arange(length, dtype=jnp.int32)[None, :]
    allowed = (col_pos <= row_pos) & (row_pos < seq_len)
    weights = jnp.where(
        allowed[None], jax.nn.silu(scores) / seq_len.astype(jnp.float32), 0.0
    ).astype(jnp.bfloat16)
    mixed_heads = jnp.einsum(
        "hij,jhe->ihe", weights, value_part, preferred_element_type=jnp.float32
    ).reshape(length, feature)
    gated_out = (layer_norm(mixed_heads, gain_mid) * gate_portion.astype(jnp.float32)).astype(
        jnp.bfloat16
    )
    result = inputs.astype(jnp.float32) + jnp.dot(
        gated_out, proj_out, preferred_element_type=jnp.float32
    )
    return jnp.where(row_pos < seq_len, result, 0.0).astype(jnp.bfloat16)


def slot_step(slot_in, seq_len, grad_out, proj_in, bias_in, gain_in, gain_mid, proj_out, toeplitz):
    result, pullback = jax.vjp(
        lambda inputs: slot_layer(
            inputs, seq_len, proj_in, bias_in, gain_in, gain_mid, proj_out, toeplitz
        ),
        slot_in,
    )
    return (result, pullback(grad_out)[0])


def selector(ids, in_range, width):
    columns = jnp.arange(width, dtype=jnp.int32)
    return ((ids[:, :, None] == columns[None, None, :]) & in_range[:, :, None]).astype(jnp.bfloat16)


def shards(
    item_table,
    unique_ids,
    inverse,
    lengths,
    assignment,
    proj_in,
    bias_in,
    gain_in,
    gain_mid,
    proj_out,
    position_bias,
    cotangent,
):
    emb_count = lax.axis_size("emb")
    seq_count = lax.axis_size("seq")
    devices = emb_count * seq_count
    rows_dev = item_table.shape[0]
    feature = item_table.shape[1]
    unique_count = unique_ids.shape[0]
    slot_cap = 2 * unique_count // devices
    owners = unique_ids // rows_dev
    local_row = unique_ids % rows_dev
    order = jnp.arange(unique_count, dtype=jnp.int32)
    earlier = (owners[:, None] == owners[None, :]) & (order[None, :] < order[:, None])
    slot_rank = jnp.sum(earlier.astype(jnp.int32), axis=1)
    request = (
        jnp.full((devices, slot_cap), rows_dev, jnp.int32).at[owners, slot_rank].set(local_row)
    )
    asked = lax.all_to_all(request, ("emb", "seq"), split_axis=0, concat_axis=0, tiled=True)
    answer = lax.all_to_all(
        item_table[jnp.minimum(asked, rows_dev - 1)],
        ("emb", "seq"),
        split_axis=0,
        concat_axis=0,
        tiled=True,
    )
    distinct_item_rows = answer[owners, slot_rank]
    slot_count = lengths.shape[0]
    per_partner = slot_count // seq_count
    max_len = inverse.shape[1]
    bucket = assignment // slot_count * per_partner + assignment % per_partner
    chosen = (
        jnp.zeros((slot_count,), jnp.int32).at[bucket].set(jnp.arange(slot_count, dtype=jnp.int32))
    )
    sent_ids = inverse[chosen]
    sent_len = lengths[chosen]
    position = jnp.arange(max_len, dtype=jnp.int32)
    toeplitz = relative_table(position_bias, max_len)
    shared = lax.all_gather(distinct_item_rows, "seq", axis=0, tiled=True)
    got_ids, count_totals = (
        lax.all_to_all(
            sent_ids.reshape(seq_count, per_partner, max_len),
            "seq",
            split_axis=0,
            concat_axis=0,
            tiled=True,
        ),
        lax.all_to_all(
            sent_len.reshape(seq_count, per_partner), "seq", split_axis=0, concat_axis=0, tiled=True
        ),
    )
    count_totals = count_totals.reshape(slot_count)
    source = jnp.arange(slot_count, dtype=jnp.int32) // per_partner
    shared_ids = got_ids.reshape(slot_count, max_len) + (source * unique_count)[:, None]
    in_range = position[None, :] < count_totals[:, None]
    row_chooser = selector(shared_ids, in_range, seq_count * unique_count)
    balanced = jnp.einsum(
        "gmq,qp->gmp", row_chooser, shared, preferred_element_type=jnp.float32
    ).astype(jnp.bfloat16)
    outputs, token_grads = lax.map(
        lambda packed: slot_step(
            packed[0], packed[1], packed[2], proj_in, bias_in, gain_in, gain_mid, proj_out, toeplitz
        ),
        (balanced, count_totals, cotangent),
    )
    partial_sums = jnp.einsum(
        "ehm,ehr->mr", row_chooser, token_grads, preferred_element_type=jnp.float32
    )
    row_gradient_list = lax.psum_scatter(
        partial_sums.astype(jnp.bfloat16), "seq", scatter_dimension=0, tiled=True
    ).astype(jnp.float32)
    outgoing_grads = (
        jnp.zeros((devices, slot_cap, feature), jnp.float32)
        .at[owners, slot_rank]
        .set(row_gradient_list)
    )
    landed = lax.all_to_all(
        outgoing_grads.astype(jnp.bfloat16), ("emb", "seq"), split_axis=0, concat_axis=0, tiled=True
    ).astype(outgoing_grads.dtype)
    table_grad = (
        jnp.zeros((rows_dev, feature), jnp.float32)
        .at[asked.reshape(-1)]
        .add(landed.reshape(-1, feature), mode="drop")
    )
    return (outputs, table_grad)


def solution(mesh):
    in_specs = (
        P(("emb", "seq"), None),
        P(("emb", "seq")),
        P(("emb", "seq"), None),
        P(("emb", "seq")),
        P(("emb", "seq")),
        P(),
        P(),
        P(),
        P(),
        P(),
        P(),
        P(("emb", "seq"), None, None),
    )
    out_specs = (P(("emb", "seq"), None, None), P(("emb", "seq"), None))
    return jax.shard_map(shards, mesh=mesh, in_specs=in_specs, out_specs=out_specs, check_vma=False)
```

```python
import functools

import jax
import jax.numpy as jnp
from jax import lax
from jax.experimental import pallas as pl
from jax.experimental.pallas import tpu as pltpu
from jax.sharding import PartitionSpec as P


def nn(a, b):
    return lax.dot_general(a, b, (((1,), (0,)), ((), ())), preferred_element_type=jnp.float32)


def nt(a, b):
    return lax.dot_general(a, b, (((1,), (1,)), ((), ())), preferred_element_type=jnp.float32)


def tn(a, b):
    return lax.dot_general(a, b, (((0,), (0,)), ((), ())), preferred_element_type=jnp.float32)


def silu_parts(values):
    gate = 0.5 * jnp.tanh(0.5 * values) + 0.5
    out = values * gate
    return out, gate + out * (1.0 - gate)


def norm_parts(values):
    center = values - jnp.mean(values, axis=-1, keepdims=True)
    spread = jnp.mean(center * center, axis=-1, keepdims=True)
    scale = lax.rsqrt(spread + 1e-05)
    return center * scale, scale


def norm_pull(grad, unit, scale):
    first = jnp.mean(grad, axis=-1, keepdims=True)
    second = jnp.mean(grad * unit, axis=-1, keepdims=True)
    return scale * (grad - first - unit * second)


def layer_kernel(
    per_source,
    unique_count,
    sel_ref,
    len_ref,
    ids_ref,
    shared_ref,
    cot_ref,
    proj_in_ref,
    bias_in_ref,
    gain_in_ref,
    gain_mid_ref,
    proj_out_ref,
    rev_ref,
    out_ref,
    part_ref,
    table,
    acc,
    hidden,
    slope,
    weights,
    wslope,
    mixed,
    dpre,
):
    step = pl.program_id(0)
    head_count, max_len = rev_ref.shape
    feature = shared_ref.shape[1]
    head = feature // head_count
    width = shared_ref.shape[0]
    root = head ** (-0.5)
    count = len_ref[step]

    @pl.when(step == 0)
    def _():
        acc[...] = jnp.zeros_like(acc)
        for h in range(head_count):
            row = jnp.broadcast_to(rev_ref[h : h + 1, :], (max_len, max_len))
            table[h] = pltpu.roll(row, 0, 1, stride=1, stride_axis=0)

    def run(rows):
        ids = ids_ref[0, :, :rows] + sel_ref[step] // per_source * unique_count
        place = lax.broadcasted_iota(jnp.int32, (1, rows), 1)
        ids = jnp.where(place < count, ids, -1)
        chooser = jnp.where(
            lax.broadcasted_iota(jnp.int32, (width, rows), 0) == ids, 1.0, 0.0
        ).astype(jnp.bfloat16)
        valid = lax.broadcasted_iota(jnp.int32, (rows, 1), 0) < count
        inputs = tn(chooser, shared_ref[...])
        unit_in, scale_in = norm_parts(inputs)
        normed = (unit_in * gain_in_ref[...]).astype(jnp.bfloat16)
        for c in range(4):
            cols = slice(c * feature, (c + 1) * feature)
            value, rate = silu_parts(nn(normed, proj_in_ref[:, cols]) + bias_in_ref[:, cols])
            hidden[:rows, cols] = value.astype(jnp.bfloat16)
            slope[:rows, cols] = rate.astype(jnp.bfloat16)
        causal = lax.broadcasted_iota(jnp.int32, (rows, rows), 1) <= lax.broadcasted_iota(
            jnp.int32, (rows, rows), 0
        )
        share = 1.0 / jnp.full((1, 1), count, jnp.int32).astype(jnp.float32)

        def part(c, h):
            return slice(c * feature + h * head, c * feature + (h + 1) * head)

        for h in range(head_count):
            score = nt(hidden[:rows, part(2, h)], hidden[:rows, part(3, h)]) * root
            value, rate = silu_parts(score + table[h, :rows, :rows])
            weight = jnp.where(causal, value * share, 0.0).astype(jnp.bfloat16)
            weights[h, :rows, :rows] = weight
            wslope[h, :rows, :rows] = jnp.where(causal, rate * share, 0.0).astype(jnp.bfloat16)
            mixed[:rows, part(0, h)] = nn(weight, hidden[:rows, part(1, h)])
        unit_mid, scale_mid = norm_parts(mixed[:rows, :])
        normed_mid = unit_mid * gain_mid_ref[...]
        gate = hidden[:rows, :feature].astype(jnp.float32)
        gated = (normed_mid * gate).astype(jnp.bfloat16)
        result = inputs + nn(gated, proj_out_ref[...])
        out_ref[0, :rows, :] = jnp.where(valid, result, 0.0).astype(jnp.bfloat16)
        if rows < max_len:
            out_ref[0, rows:, :] = jnp.zeros((max_len - rows, feature), jnp.bfloat16)

        grad = jnp.where(valid, cot_ref[0, :rows, :].astype(jnp.float32), 0.0)
        grad_gated = nt(grad.astype(jnp.bfloat16), proj_out_ref[...])
        grad_gated = grad_gated.astype(jnp.bfloat16).astype(jnp.float32)

        def put(cols, value):
            value = value.astype(jnp.bfloat16).astype(jnp.float32)
            dpre[:rows, cols] = (value * slope[:rows, cols].astype(jnp.float32)).astype(
                jnp.bfloat16
            )

        put(slice(0, feature), grad_gated * normed_mid)
        grad_mixed = norm_pull(grad_gated * gate * gain_mid_ref[...], unit_mid, scale_mid)
        grad_mixed = grad_mixed.astype(jnp.bfloat16)
        for h in range(head_count):
            grad_head = grad_mixed[:, h * head : (h + 1) * head]
            put(part(1, h), tn(weights[h, :rows, :rows], grad_head))
            grad_weight = nt(grad_head, hidden[:rows, part(1, h)])
            grad_score = (grad_weight * wslope[h, :rows, :rows].astype(jnp.float32)).astype(
                jnp.bfloat16
            )
            put(part(2, h), nn(grad_score, hidden[:rows, part(3, h)]) * root)
            put(part(3, h), tn(grad_score, hidden[:rows, part(2, h)]) * root)
        grad_normed = nt(dpre[:rows, :], proj_in_ref[...])
        grad_normed = grad_normed.astype(jnp.bfloat16).astype(jnp.float32)
        grad_in = norm_pull(grad_normed * gain_in_ref[...], unit_in, scale_in)
        token_grad = (grad_in.astype(jnp.bfloat16).astype(jnp.float32) + grad).astype(jnp.bfloat16)
        acc[...] += nn(chooser, token_grad)

    half = max_len // 2

    @pl.when(count <= half)
    def _():
        run(half)

    @pl.when(count > half)
    def _():
        run(max_len)

    @pl.when(step == pl.num_programs(0) - 1)
    def _():
        part_ref[...] = acc[...].astype(part_ref.dtype)


def layers(
    selected, counts, ids, shared, cotangent, proj_in, bias_in, gain_in, gain_mid, proj_out, position_bias, per_source, unique_count
):
    slots, max_len, feature = cotangent.shape
    heads = position_bias.shape[0]
    width = shared.shape[0]
    rev = jnp.concatenate([position_bias[:, :1], position_bias[:, :0:-1]], axis=1)
    whole = lambda shape: pl.BlockSpec(shape, lambda t, sel, n: (0,) * len(shape))
    slot = pl.BlockSpec((1, max_len, feature), lambda t, sel, n: (t, 0, 0))
    return pl.pallas_call(
        functools.partial(layer_kernel, per_source, unique_count),
        grid_spec=pltpu.PrefetchScalarGridSpec(
            num_scalar_prefetch=2,
            grid=(slots,),
            in_specs=[
                pl.BlockSpec((1, 1, max_len), lambda t, sel, n: (sel[t], 0, 0)),
                whole((width, feature)),
                slot,
                whole(proj_in.shape),
                whole((1, bias_in.shape[0])),
                whole((1, feature)),
                whole((1, feature)),
                whole(proj_out.shape),
                whole((heads, max_len)),
            ],
            out_specs=[slot, whole((width, feature))],
            scratch_shapes=[
                pltpu.VMEM((heads, max_len, max_len), jnp.float32),
                pltpu.VMEM((width, feature), jnp.float32),
                pltpu.VMEM((max_len, 4 * feature), jnp.bfloat16),
                pltpu.VMEM((max_len, 4 * feature), jnp.bfloat16),
                pltpu.VMEM((heads, max_len, max_len), jnp.bfloat16),
                pltpu.VMEM((heads, max_len, max_len), jnp.bfloat16),
                pltpu.VMEM((max_len, feature), jnp.float32),
                pltpu.VMEM((max_len, 4 * feature), jnp.bfloat16),
            ],
        ),
        out_shape=[
            jax.ShapeDtypeStruct((slots, max_len, feature), jnp.bfloat16),
            jax.ShapeDtypeStruct((width, feature), jnp.bfloat16),
        ],
        compiler_params=pltpu.CompilerParams(
            dimension_semantics=("arbitrary",), vmem_limit_bytes=48 * 1024 * 1024
        ),
    )(
        selected, counts, ids.reshape(ids.shape[0], 1, max_len), shared, cotangent,
        proj_in, bias_in[None], gain_in[None], gain_mid[None], proj_out, rev,
    )


def shards(
    item_table,
    unique_ids,
    inverse,
    lengths,
    assignment,
    proj_in,
    bias_in,
    gain_in,
    gain_mid,
    proj_out,
    position_bias,
    cotangent,
):
    emb_count = lax.axis_size("emb")
    seq_count = lax.axis_size("seq")
    devices = emb_count * seq_count
    rows_dev = item_table.shape[0]
    feature = item_table.shape[1]
    unique_count = unique_ids.shape[0]
    slot_cap = 2 * unique_count // devices
    owners = unique_ids // rows_dev
    local_row = unique_ids % rows_dev
    order = jnp.arange(unique_count, dtype=jnp.int32)
    earlier = (owners[:, None] == owners[None, :]) & (order[None, :] < order[:, None])
    slot_rank = jnp.sum(earlier.astype(jnp.int32), axis=1)
    request = (
        jnp.full((devices, slot_cap), rows_dev, jnp.int32).at[owners, slot_rank].set(local_row)
    )
    asked = lax.all_to_all(request, ("emb", "seq"), split_axis=0, concat_axis=0, tiled=True)
    answer = lax.all_to_all(
        item_table[jnp.minimum(asked, rows_dev - 1)],
        ("emb", "seq"),
        split_axis=0,
        concat_axis=0,
        tiled=True,
    )
    distinct_item_rows = answer[owners, slot_rank]
    slot_count = lengths.shape[0]
    max_len = inverse.shape[1]
    packed = jnp.concatenate([inverse, lengths[:, None], assignment[:, None]], axis=1)
    group = lax.all_gather(packed, "seq", axis=0, tiled=True)
    group_ids = group[:, :max_len]
    group_len = group[:, max_len]
    mine = lax.axis_index("seq") * slot_count + jnp.arange(slot_count, dtype=jnp.int32)
    hit = (group[:, max_len + 1][None, :] == mine[:, None]).astype(jnp.int32)
    selected = jnp.sum(hit * jnp.arange(hit.shape[1], dtype=jnp.int32)[None, :], axis=1)
    counts = jnp.sum(hit * group_len[None, :], axis=1)
    shared = lax.all_gather(distinct_item_rows, "seq", axis=0, tiled=True)
    outputs, partial_sums = layers(
        selected, counts, group_ids, shared, cotangent, proj_in, bias_in, gain_in, gain_mid,
        proj_out, position_bias, slot_count, unique_count,
    )
    pieces = lax.all_to_all(partial_sums, "seq", split_axis=0, concat_axis=0, tiled=True)
    row_gradient_list = jnp.sum(
        pieces.reshape(seq_count, unique_count, feature).astype(jnp.float32), axis=0
    )
    outgoing_grads = (
        jnp.zeros((devices, slot_cap, feature), jnp.float32)
        .at[owners, slot_rank]
        .set(row_gradient_list)
    )
    landed = lax.all_to_all(
        outgoing_grads.astype(jnp.bfloat16), ("emb", "seq"), split_axis=0, concat_axis=0, tiled=True
    ).astype(outgoing_grads.dtype)
    table_grad = (
        jnp.zeros((rows_dev, feature), jnp.float32)
        .at[asked.reshape(-1)]
        .add(landed.reshape(-1, feature), mode="drop")
    )
    return (outputs, table_grad)


def solution(mesh):
    in_specs = (
        P(("emb", "seq"), None),
        P(("emb", "seq")),
        P(("emb", "seq"), None),
        P(("emb", "seq")),
        P(("emb", "seq")),
        P(),
        P(),
        P(),
        P(),
        P(),
        P(),
        P(("emb", "seq"), None, None),
    )
    out_specs = (P(("emb", "seq"), None, None), P(("emb", "seq"), None))
    return jax.shard_map(shards, mesh=mesh, in_specs=in_specs, out_specs=out_specs, check_vma=False)
```

```python
import functools

import jax
import jax.numpy as jnp
from jax import lax
from jax.experimental import pallas as pl
from jax.experimental.pallas import tpu as pltpu
from jax.sharding import PartitionSpec as P


def nn(a, b):
    return lax.dot_general(a, b, (((1,), (0,)), ((), ())), preferred_element_type=jnp.float32)


def nt(a, b):
    return lax.dot_general(a, b, (((1,), (1,)), ((), ())), preferred_element_type=jnp.float32)


def tn(a, b):
    return lax.dot_general(a, b, (((0,), (0,)), ((), ())), preferred_element_type=jnp.float32)


def silu_parts(values):
    gate = 0.5 * jnp.tanh(0.5 * values) + 0.5
    out = values * gate
    return out, gate + out * (1.0 - gate)


def norm_parts(values):
    center = values - jnp.mean(values, axis=-1, keepdims=True)
    spread = jnp.mean(center * center, axis=-1, keepdims=True)
    scale = lax.rsqrt(spread + 1e-05)
    return center * scale, scale


def norm_pull(grad, unit, scale):
    first = jnp.mean(grad, axis=-1, keepdims=True)
    second = jnp.mean(grad * unit, axis=-1, keepdims=True)
    return scale * (grad - first - unit * second)


def layer_kernel(
    per_source,
    unique_count,
    bundle,
    sel_ref,
    len_ref,
    *refs,
):
    ids_refs = refs[:bundle]
    (
        shared_ref, cot_ref, proj_in_ref, bias_in_ref, gain_in_ref, gain_mid_ref, proj_out_ref,
        rev_ref, out_ref, part_ref, table, acc, hidden, slope, weights, wslope, mixed, dpre,
    ) = refs[bundle:]
    step = pl.program_id(0)
    head_count, max_len = rev_ref.shape
    feature = shared_ref.shape[1]
    head = feature // head_count
    width = shared_ref.shape[0]
    root = head ** (-0.5)
    slots = [step * bundle + b for b in range(bundle)]
    counts = [len_ref[t] for t in slots]
    longest = functools.reduce(jnp.maximum, counts)

    @pl.when(step == 0)
    def _():
        acc[...] = jnp.zeros_like(acc)
        for h in range(head_count):
            row = jnp.broadcast_to(rev_ref[h : h + 1, :], (max_len, max_len))
            table[h] = pltpu.roll(row, 0, 1, stride=1, stride_axis=0)

    def run(rows):
        total = bundle * rows
        spans = [slice(b * rows, (b + 1) * rows) for b in range(bundle)]
        place = lax.broadcasted_iota(jnp.int32, (1, rows), 1)
        ids = jnp.concatenate(
            [
                jnp.where(
                    place < n, ref[0, :, :rows] + sel_ref[t] // per_source * unique_count, -1
                )
                for ref, t, n in zip(ids_refs, slots, counts)
            ],
            axis=1,
        )
        chooser = jnp.where(
            lax.broadcasted_iota(jnp.int32, (width, total), 0) == ids, 1.0, 0.0
        ).astype(jnp.bfloat16)
        row = lax.broadcasted_iota(jnp.int32, (rows, 1), 0)
        valid = jnp.concatenate([(row < n).astype(jnp.float32) for n in counts], axis=0) > 0.5
        inputs = tn(chooser, shared_ref[...])
        unit_in, scale_in = norm_parts(inputs)
        normed = (unit_in * gain_in_ref[...]).astype(jnp.bfloat16)
        for c in (2, 3, 1, 0):
            cols = slice(c * feature, (c + 1) * feature)
            value, rate = silu_parts(nn(normed, proj_in_ref[:, cols]) + bias_in_ref[:, cols])
            hidden[:total, cols] = value.astype(jnp.bfloat16)
            slope[:total, cols] = rate.astype(jnp.bfloat16)
        causal = lax.broadcasted_iota(jnp.int32, (rows, rows), 1) <= lax.broadcasted_iota(
            jnp.int32, (rows, rows), 0
        )

        def part(c, h):
            return slice(c * feature + h * head, c * feature + (h + 1) * head)

        for b, span in enumerate(spans):
            share = 1.0 / jnp.full((1, 1), counts[b], jnp.int32).astype(jnp.float32)
            causal_share = jnp.where(causal, share, 0.0)
            for h in range(head_count):
                score = nt(hidden[span, part(2, h)], hidden[span, part(3, h)]) * root
                value, rate = silu_parts(score + table[h, :rows, :rows])
                weight = (value * causal_share).astype(jnp.bfloat16)
                weights[b, h, :rows, :rows] = weight
                wslope[b, h, :rows, :rows] = (rate * causal_share).astype(jnp.bfloat16)
                mixed[span, part(0, h)] = nn(weight, hidden[span, part(1, h)])
        unit_mid, scale_mid = norm_parts(mixed[:total, :])
        normed_mid = unit_mid * gain_mid_ref[...]
        gate = hidden[:total, :feature].astype(jnp.float32)
        gated = (normed_mid * gate).astype(jnp.bfloat16)
        result = inputs + nn(gated, proj_out_ref[...])
        result = jnp.where(valid, result, 0.0).astype(jnp.bfloat16)
        for b, span in enumerate(spans):
            out_ref[b, :rows, :] = result[span, :]
            if rows < max_len:
                out_ref[b, rows:, :] = jnp.zeros((max_len - rows, feature), jnp.bfloat16)

        grad = jnp.concatenate([cot_ref[b, :rows, :] for b in range(bundle)], axis=0)
        grad = jnp.where(valid, grad.astype(jnp.float32), 0.0)
        grad_gated = nt(grad.astype(jnp.bfloat16), proj_out_ref[...])
        grad_gated = grad_gated.astype(jnp.bfloat16).astype(jnp.float32)

        def put(span, cols, value):
            value = value.astype(jnp.bfloat16).astype(jnp.float32)
            dpre[span, cols] = (value * slope[span, cols].astype(jnp.float32)).astype(
                jnp.bfloat16
            )

        put(slice(0, total), slice(0, feature), grad_gated * normed_mid)
        grad_mixed = norm_pull(grad_gated * gate * gain_mid_ref[...], unit_mid, scale_mid)
        grad_mixed = grad_mixed.astype(jnp.bfloat16)
        for b, span in enumerate(spans):
            for h in range(head_count):
                grad_head = grad_mixed[span, h * head : (h + 1) * head]
                put(span, part(1, h), tn(weights[b, h, :rows, :rows], grad_head))
                grad_weight = nt(grad_head, hidden[span, part(1, h)])
                grad_score = (
                    grad_weight * wslope[b, h, :rows, :rows].astype(jnp.float32)
                ).astype(jnp.bfloat16)
                put(span, part(2, h), nn(grad_score, hidden[span, part(3, h)]) * root)
                put(span, part(3, h), tn(grad_score, hidden[span, part(2, h)]) * root)
        grad_normed = nt(dpre[:total, :], proj_in_ref[...])
        grad_normed = grad_normed.astype(jnp.bfloat16).astype(jnp.float32)
        grad_in = norm_pull(grad_normed * gain_in_ref[...], unit_in, scale_in)
        token_grad = (grad_in.astype(jnp.bfloat16).astype(jnp.float32) + grad).astype(jnp.bfloat16)
        acc[...] += nn(chooser, token_grad)

    half = max_len // 2

    @pl.when(longest <= half)
    def _():
        run(half)

    @pl.when(longest > half)
    def _():
        run(max_len)

    @pl.when(step == pl.num_programs(0) - 1)
    def _():
        part_ref[...] = acc[...].astype(part_ref.dtype)


def layers(
    selected, counts, ids, shared, cotangent, proj_in, bias_in, gain_in, gain_mid, proj_out, position_bias, per_source, unique_count, bundle
):
    slots, max_len, feature = cotangent.shape
    heads = position_bias.shape[0]
    width = shared.shape[0]
    rev = jnp.concatenate([position_bias[:, :1], position_bias[:, :0:-1]], axis=1)
    whole = lambda shape: pl.BlockSpec(shape, lambda t, sel, n: (0,) * len(shape))
    slot = pl.BlockSpec((bundle, max_len, feature), lambda t, sel, n: (t, 0, 0))
    ids = ids.reshape(ids.shape[0], 1, max_len)

    def chosen(b):
        return pl.BlockSpec((1, 1, max_len), lambda t, sel, n: (sel[t * bundle + b], 0, 0))
    return pl.pallas_call(
        functools.partial(layer_kernel, per_source, unique_count, bundle),
        grid_spec=pltpu.PrefetchScalarGridSpec(
            num_scalar_prefetch=2,
            grid=(slots // bundle,),
            in_specs=[
                *[chosen(b) for b in range(bundle)],
                whole((width, feature)),
                slot,
                whole(proj_in.shape),
                whole((1, bias_in.shape[0])),
                whole((1, feature)),
                whole((1, feature)),
                whole(proj_out.shape),
                whole((heads, max_len)),
            ],
            out_specs=[slot, whole((width, feature))],
            scratch_shapes=[
                pltpu.VMEM((heads, max_len, max_len), jnp.float32),
                pltpu.VMEM((width, feature), jnp.float32),
                pltpu.VMEM((bundle * max_len, 4 * feature), jnp.bfloat16),
                pltpu.VMEM((bundle * max_len, 4 * feature), jnp.bfloat16),
                pltpu.VMEM((bundle, heads, max_len, max_len), jnp.bfloat16),
                pltpu.VMEM((bundle, heads, max_len, max_len), jnp.bfloat16),
                pltpu.VMEM((bundle * max_len, feature), jnp.float32),
                pltpu.VMEM((bundle * max_len, 4 * feature), jnp.bfloat16),
            ],
        ),
        out_shape=[
            jax.ShapeDtypeStruct((slots, max_len, feature), jnp.bfloat16),
            jax.ShapeDtypeStruct((width, feature), jnp.bfloat16),
        ],
        compiler_params=pltpu.CompilerParams(
            dimension_semantics=("arbitrary",), vmem_limit_bytes=48 * 1024 * 1024
        ),
    )(
        selected, counts, *[ids] * bundle, shared, cotangent,
        proj_in, bias_in[None], gain_in[None], gain_mid[None], proj_out, rev,
    )


def shards(
    item_table,
    unique_ids,
    inverse,
    lengths,
    assignment,
    proj_in,
    bias_in,
    gain_in,
    gain_mid,
    proj_out,
    position_bias,
    cotangent,
):
    emb_count = lax.axis_size("emb")
    seq_count = lax.axis_size("seq")
    devices = emb_count * seq_count
    rows_dev = item_table.shape[0]
    feature = item_table.shape[1]
    unique_count = unique_ids.shape[0]
    slot_cap = 2 * unique_count // devices
    owners = unique_ids // rows_dev
    local_row = unique_ids % rows_dev
    order = jnp.arange(unique_count, dtype=jnp.int32)
    earlier = (owners[:, None] == owners[None, :]) & (order[None, :] < order[:, None])
    slot_rank = jnp.sum(earlier.astype(jnp.int32), axis=1)
    spot = owners * slot_cap + slot_rank
    spots = jnp.arange(devices * slot_cap, dtype=jnp.int32)
    placed = spots[:, None] == spot[None, :]
    request = rows_dev + jnp.sum(
        jnp.where(placed, local_row[None, :] - rows_dev, 0), axis=1
    ).reshape(devices, slot_cap)
    asked = lax.all_to_all(request, ("emb", "seq"), split_axis=0, concat_axis=0, tiled=True)
    answer = lax.all_to_all(
        item_table[jnp.minimum(asked, rows_dev - 1)],
        ("emb", "seq"),
        split_axis=0,
        concat_axis=0,
        tiled=True,
    )
    distinct_item_rows = answer[owners, slot_rank]
    slot_count = lengths.shape[0]
    max_len = inverse.shape[1]
    packed = jnp.concatenate([inverse, lengths[:, None], assignment[:, None]], axis=1)
    group = lax.all_gather(packed, "seq", axis=0, tiled=True)
    group_ids = group[:, :max_len]
    group_len = group[:, max_len]
    mine = lax.axis_index("seq") * slot_count + jnp.arange(slot_count, dtype=jnp.int32)
    hit = (group[:, max_len + 1][None, :] == mine[:, None]).astype(jnp.int32)
    selected = jnp.sum(hit * jnp.arange(hit.shape[1], dtype=jnp.int32)[None, :], axis=1)
    counts = jnp.sum(hit * group_len[None, :], axis=1)
    shared = lax.all_gather(distinct_item_rows, "seq", axis=0, tiled=True)
    outputs, partial_sums = layers(
        selected, counts, group_ids, shared, cotangent, proj_in, bias_in, gain_in, gain_mid,
        proj_out, position_bias, slot_count, unique_count, max(slot_count // seq_count, 1),
    )
    pieces = lax.all_to_all(partial_sums, "seq", split_axis=0, concat_axis=0, tiled=True)
    row_gradient_list = jnp.sum(
        pieces.reshape(seq_count, unique_count, feature).astype(jnp.float32), axis=0
    )
    outgoing_grads = jnp.dot(
        placed.astype(jnp.bfloat16),
        row_gradient_list.astype(jnp.bfloat16),
        preferred_element_type=jnp.float32,
    ).astype(jnp.bfloat16)
    landed = lax.all_to_all(
        outgoing_grads.reshape(devices, slot_cap, feature),
        ("emb", "seq"),
        split_axis=0,
        concat_axis=0,
        tiled=True,
    )
    holder = jnp.arange(rows_dev, dtype=jnp.int32)[:, None] == asked.reshape(1, -1)
    table_grad = jnp.dot(
        holder.astype(jnp.bfloat16),
        landed.reshape(-1, feature),
        preferred_element_type=jnp.float32,
    )
    return (outputs, table_grad)


def solution(mesh):
    in_specs = (
        P(("emb", "seq"), None),
        P(("emb", "seq")),
        P(("emb", "seq"), None),
        P(("emb", "seq")),
        P(("emb", "seq")),
        P(),
        P(),
        P(),
        P(),
        P(),
        P(),
        P(("emb", "seq"), None, None),
    )
    out_specs = (P(("emb", "seq"), None, None), P(("emb", "seq"), None))
    return jax.shard_map(shards, mesh=mesh, in_specs=in_specs, out_specs=out_specs, check_vma=False)
```

```python
import functools

import jax
import jax.numpy as jnp
from jax import lax
from jax.experimental import pallas as pl
from jax.experimental.pallas import tpu as pltpu
from jax.sharding import PartitionSpec as P


def nn(a, b):
    return lax.dot_general(a, b, (((1,), (0,)), ((), ())), preferred_element_type=jnp.float32)


def nt(a, b):
    return lax.dot_general(a, b, (((1,), (1,)), ((), ())), preferred_element_type=jnp.float32)


def tn(a, b):
    return lax.dot_general(a, b, (((0,), (0,)), ((), ())), preferred_element_type=jnp.float32)


def silu_parts(values):
    gate = 0.5 * jnp.tanh(0.5 * values) + 0.5
    out = values * gate
    return out, gate + out * (1.0 - gate)


def norm_parts(values):
    center = values - jnp.mean(values, axis=-1, keepdims=True)
    spread = jnp.mean(center * center, axis=-1, keepdims=True)
    scale = lax.rsqrt(spread + 1e-05)
    return center * scale, scale


def norm_pull(grad, unit, scale):
    first = jnp.mean(grad, axis=-1, keepdims=True)
    second = jnp.mean(grad * unit, axis=-1, keepdims=True)
    return scale * (grad - first - unit * second)


def layer_kernel(
    per_source,
    unique_count,
    bundle,
    sel_ref,
    len_ref,
    *refs,
):
    ids_refs = refs[:bundle]
    (
        shared_ref, cot_ref, proj_in_ref, bias_in_ref, gain_in_ref, gain_mid_ref, proj_out_ref,
        rev_ref, out_ref, part_ref, table, acc, hidden, slope, weights, wslope, mixed, dpre,
    ) = refs[bundle:]
    step = pl.program_id(0)
    head_count, max_len = rev_ref.shape
    feature = shared_ref.shape[1]
    head = feature // head_count
    width = shared_ref.shape[0]
    root = head ** (-0.5)
    slots = [step * bundle + b for b in range(bundle)]
    counts = [len_ref[t] for t in slots]
    longest = functools.reduce(jnp.maximum, counts)

    @pl.when(step == 0)
    def _():
        acc[...] = jnp.zeros_like(acc)
        for h in range(head_count):
            row = jnp.broadcast_to(rev_ref[h : h + 1, :], (max_len, max_len))
            table[h] = pltpu.roll(row, 0, 1, stride=1, stride_axis=0)

    def run(rows):
        total = bundle * rows
        spans = [slice(b * rows, (b + 1) * rows) for b in range(bundle)]
        place = lax.broadcasted_iota(jnp.int32, (1, rows), 1)
        ids = jnp.concatenate(
            [
                jnp.where(
                    place < n, ref[0, :, :rows] + sel_ref[t] // per_source * unique_count, -1
                )
                for ref, t, n in zip(ids_refs, slots, counts)
            ],
            axis=1,
        )
        chooser = jnp.where(
            lax.broadcasted_iota(jnp.int32, (width, total), 0) == ids, 1.0, 0.0
        ).astype(jnp.bfloat16)
        row = lax.broadcasted_iota(jnp.int32, (rows, 1), 0)
        valid = jnp.concatenate([(row < n).astype(jnp.float32) for n in counts], axis=0) > 0.5
        inputs = tn(chooser, shared_ref[...])
        unit_in, scale_in = norm_parts(inputs)
        normed = (unit_in * gain_in_ref[...]).astype(jnp.bfloat16)
        for c in (2, 3, 1, 0):
            cols = slice(c * feature, (c + 1) * feature)
            value, rate = silu_parts(nn(normed, proj_in_ref[:, cols]) + bias_in_ref[:, cols])
            hidden[:total, cols] = value.astype(jnp.bfloat16)
            slope[:total, cols] = rate.astype(jnp.bfloat16)
        causal = lax.broadcasted_iota(jnp.int32, (rows, rows), 1) <= lax.broadcasted_iota(
            jnp.int32, (rows, rows), 0
        )

        def part(c, h):
            return slice(c * feature + h * head, c * feature + (h + 1) * head)

        for b, span in enumerate(spans):
            share = 1.0 / jnp.full((1, 1), counts[b], jnp.int32).astype(jnp.float32)
            causal_share = jnp.where(causal, share, 0.0)
            for h in range(head_count):
                score = nt(hidden[span, part(2, h)], hidden[span, part(3, h)]) * root
                value, rate = silu_parts(score + table[h, :rows, :rows])
                weight = (value * causal_share).astype(jnp.bfloat16)
                weights[b, h, :rows, :rows] = weight
                wslope[b, h, :rows, :rows] = (rate * causal_share).astype(jnp.bfloat16)
                mixed[span, part(0, h)] = nn(weight, hidden[span, part(1, h)])
        unit_mid, scale_mid = norm_parts(mixed[:total, :])
        normed_mid = unit_mid * gain_mid_ref[...]
        gate = hidden[:total, :feature].astype(jnp.float32)
        gated = (normed_mid * gate).astype(jnp.bfloat16)
        result = inputs + nn(gated, proj_out_ref[...])
        result = jnp.where(valid, result, 0.0).astype(jnp.bfloat16)
        for b, span in enumerate(spans):
            out_ref[b, :rows, :] = result[span, :]
            if rows < max_len:
                out_ref[b, rows:, :] = jnp.zeros((max_len - rows, feature), jnp.bfloat16)

        grad = jnp.concatenate([cot_ref[b, :rows, :] for b in range(bundle)], axis=0)
        grad = jnp.where(valid, grad.astype(jnp.float32), 0.0)
        grad_gated = nt(grad.astype(jnp.bfloat16), proj_out_ref[...])
        grad_gated = grad_gated.astype(jnp.bfloat16).astype(jnp.float32)

        def put(span, cols, value):
            value = value.astype(jnp.bfloat16).astype(jnp.float32)
            dpre[span, cols] = (value * slope[span, cols].astype(jnp.float32)).astype(
                jnp.bfloat16
            )

        put(slice(0, total), slice(0, feature), grad_gated * normed_mid)
        grad_mixed = norm_pull(grad_gated * gate * gain_mid_ref[...], unit_mid, scale_mid)
        grad_mixed = grad_mixed.astype(jnp.bfloat16)
        for b, span in enumerate(spans):
            for h in range(head_count):
                grad_head = grad_mixed[span, h * head : (h + 1) * head]
                put(span, part(1, h), tn(weights[b, h, :rows, :rows], grad_head))
                grad_weight = nt(grad_head, hidden[span, part(1, h)])
                grad_score = (
                    grad_weight * wslope[b, h, :rows, :rows].astype(jnp.float32)
                ).astype(jnp.bfloat16)
                put(span, part(2, h), nn(grad_score, hidden[span, part(3, h)]) * root)
                put(span, part(3, h), tn(grad_score, hidden[span, part(2, h)]) * root)
        grad_normed = nt(dpre[:total, :], proj_in_ref[...])
        grad_normed = grad_normed.astype(jnp.bfloat16).astype(jnp.float32)
        grad_in = norm_pull(grad_normed * gain_in_ref[...], unit_in, scale_in)
        token_grad = (grad_in.astype(jnp.bfloat16).astype(jnp.float32) + grad).astype(jnp.bfloat16)
        acc[...] += nn(chooser, token_grad)

    half = max_len // 2

    @pl.when(longest <= half)
    def _():
        run(half)

    @pl.when(longest > half)
    def _():
        run(max_len)

    @pl.when(step == pl.num_programs(0) - 1)
    def _():
        part_ref[...] = acc[...].astype(part_ref.dtype)


def layers(
    selected, counts, ids, shared, cotangent, proj_in, bias_in, gain_in, gain_mid, proj_out, position_bias, per_source, unique_count, bundle
):
    slots, max_len, feature = cotangent.shape
    heads = position_bias.shape[0]
    width = shared.shape[0]
    rev = jnp.concatenate([position_bias[:, :1], position_bias[:, :0:-1]], axis=1)
    whole = lambda shape: pl.BlockSpec(shape, lambda t, sel, n: (0,) * len(shape))
    slot = pl.BlockSpec((bundle, max_len, feature), lambda t, sel, n: (t, 0, 0))
    ids = ids.reshape(ids.shape[0], 1, max_len)

    def chosen(b):
        return pl.BlockSpec((1, 1, max_len), lambda t, sel, n: (sel[t * bundle + b], 0, 0))
    return pl.pallas_call(
        functools.partial(layer_kernel, per_source, unique_count, bundle),
        grid_spec=pltpu.PrefetchScalarGridSpec(
            num_scalar_prefetch=2,
            grid=(slots // bundle,),
            in_specs=[
                *[chosen(b) for b in range(bundle)],
                whole((width, feature)),
                slot,
                whole(proj_in.shape),
                whole((1, bias_in.shape[0])),
                whole((1, feature)),
                whole((1, feature)),
                whole(proj_out.shape),
                whole((heads, max_len)),
            ],
            out_specs=[slot, whole((width, feature))],
            scratch_shapes=[
                pltpu.VMEM((heads, max_len, max_len), jnp.float32),
                pltpu.VMEM((width, feature), jnp.float32),
                pltpu.VMEM((bundle * max_len, 4 * feature), jnp.bfloat16),
                pltpu.VMEM((bundle * max_len, 4 * feature), jnp.bfloat16),
                pltpu.VMEM((bundle, heads, max_len, max_len), jnp.bfloat16),
                pltpu.VMEM((bundle, heads, max_len, max_len), jnp.bfloat16),
                pltpu.VMEM((bundle * max_len, feature), jnp.float32),
                pltpu.VMEM((bundle * max_len, 4 * feature), jnp.bfloat16),
            ],
        ),
        out_shape=[
            jax.ShapeDtypeStruct((slots, max_len, feature), jnp.bfloat16),
            jax.ShapeDtypeStruct((width, feature), jnp.bfloat16),
        ],
        compiler_params=pltpu.CompilerParams(
            dimension_semantics=("arbitrary",), vmem_limit_bytes=48 * 1024 * 1024
        ),
    )(
        selected, counts, *[ids] * bundle, shared, cotangent,
        proj_in, bias_in[None], gain_in[None], gain_mid[None], proj_out, rev,
    )


def shards(
    item_table,
    unique_ids,
    inverse,
    lengths,
    assignment,
    proj_in,
    bias_in,
    gain_in,
    gain_mid,
    proj_out,
    position_bias,
    cotangent,
):
    emb_count = lax.axis_size("emb")
    seq_count = lax.axis_size("seq")
    devices = emb_count * seq_count
    rows_dev = item_table.shape[0]
    feature = item_table.shape[1]
    unique_count = unique_ids.shape[0]
    slot_cap = 2 * unique_count // devices
    owners = unique_ids // rows_dev
    local_row = unique_ids % rows_dev
    order = jnp.arange(unique_count, dtype=jnp.int32)
    earlier = (owners[:, None] == owners[None, :]) & (order[None, :] < order[:, None])
    slot_rank = jnp.sum(earlier.astype(jnp.int32), axis=1)
    spot = owners * slot_cap + slot_rank
    spots = jnp.arange(devices * slot_cap, dtype=jnp.int32)
    placed = spots[:, None] == spot[None, :]
    request = rows_dev + jnp.sum(
        jnp.where(placed, local_row[None, :] - rows_dev, 0), axis=1
    ).reshape(devices, slot_cap)
    asked = lax.all_to_all(request, ("emb", "seq"), split_axis=0, concat_axis=0, tiled=True)
    answer = lax.all_to_all(
        item_table[jnp.minimum(asked, rows_dev - 1)],
        ("emb", "seq"),
        split_axis=0,
        concat_axis=0,
        tiled=True,
    )
    distinct_item_rows = answer[owners, slot_rank]
    slot_count = lengths.shape[0]
    max_len = inverse.shape[1]
    numbers = jnp.concatenate([inverse.reshape(-1), lengths, assignment]).astype(jnp.bfloat16)
    extra = -(-numbers.shape[0] // (16 * feature)) * 16
    numbers = jnp.pad(numbers, (0, extra * feature - numbers.shape[0]))
    packed = jnp.concatenate([distinct_item_rows, numbers.reshape(extra, feature)], axis=0)
    group = lax.all_gather(packed, "seq", axis=0, tiled=False)
    shared = group[:, :unique_count].reshape(seq_count * unique_count, feature)
    numbers = group[:, unique_count:].reshape(seq_count, extra * feature).astype(jnp.int32)
    tokens = slot_count * max_len
    group_ids = numbers[:, :tokens].reshape(seq_count * slot_count, max_len)
    group_len = numbers[:, tokens : tokens + slot_count].reshape(-1)
    group_place = numbers[:, tokens + slot_count : tokens + 2 * slot_count].reshape(-1)
    mine = lax.axis_index("seq") * slot_count + jnp.arange(slot_count, dtype=jnp.int32)
    hit = (group_place[None, :] == mine[:, None]).astype(jnp.int32)
    selected = jnp.sum(hit * jnp.arange(hit.shape[1], dtype=jnp.int32)[None, :], axis=1)
    counts = jnp.sum(hit * group_len[None, :], axis=1)
    outputs, partial_sums = layers(
        selected, counts, group_ids, shared, cotangent, proj_in, bias_in, gain_in, gain_mid,
        proj_out, position_bias, slot_count, unique_count, max(slot_count // seq_count, 1),
    )
    pieces = lax.all_to_all(partial_sums, "seq", split_axis=0, concat_axis=0, tiled=True)
    row_gradient_list = jnp.sum(
        pieces.reshape(seq_count, unique_count, feature).astype(jnp.float32), axis=0
    )
    outgoing_grads = jnp.dot(
        placed.astype(jnp.bfloat16),
        row_gradient_list.astype(jnp.bfloat16),
        preferred_element_type=jnp.float32,
    ).astype(jnp.bfloat16)
    landed = lax.all_to_all(
        outgoing_grads.reshape(devices, slot_cap, feature),
        ("emb", "seq"),
        split_axis=0,
        concat_axis=0,
        tiled=True,
    )
    holder = jnp.arange(rows_dev, dtype=jnp.int32)[:, None] == asked.reshape(1, -1)
    table_grad = jnp.dot(
        holder.astype(jnp.bfloat16),
        landed.reshape(-1, feature),
        preferred_element_type=jnp.float32,
    )
    return (outputs, table_grad)


def solution(mesh):
    in_specs = (
        P(("emb", "seq"), None),
        P(("emb", "seq")),
        P(("emb", "seq"), None),
        P(("emb", "seq")),
        P(("emb", "seq")),
        P(),
        P(),
        P(),
        P(),
        P(),
        P(),
        P(("emb", "seq"), None, None),
    )
    out_specs = (P(("emb", "seq"), None, None), P(("emb", "seq"), None))
    return jax.shard_map(shards, mesh=mesh, in_specs=in_specs, out_specs=out_specs, check_vma=False)
```
